32 devices in a mesh: tm: 4 (over x, core), space: 8 (over z, y).
Axes of the slice: x: 2, y: 2, z: 4, core: 2. Of those that a mesh axis runs over, the one named last changes fastest.
Arguments:
- field: float32 [2048, 128, 256], P('tm', 'space'), may hold values from -6 to 6
- mask: int32 [2048, 128, 256], P('tm', 'space'), may hold values 0 or 1
- noise: float32 [128, 256], P('space'), may hold values from 0.1 to 1
- lat_factor: float32 [128, 128], replicated, may hold values from -1 to 2.5, as said below
- lon_factor: float32 [256, 256], replicated, may hold values from -1 to 2.5, as said below
- time_tiles: float32 [5, 128, 128], replicated, may hold values from -1 to 2.5, as said below
- amplitude: float32 [16], replicated, may hold values from 0.5 to 2
- depth: int32 [16], replicated, may hold values from 0 to 4
Outputs:
- product: float32 [2048, 128, 256], P('tm', 'space')
The draws below stay inside these ranges and needn't reach their ends.
Inputs may be any that keep to these rules, and one draw needn't show every extreme that they name: `lat_factor`: symmetric. `lon_factor`: symmetric. time_tiles[0] is symmetric.
All inputs are finite; a program needn't handle non-finite values. No bound on the sum of `mask` on one device may be relied on, other than what follows from the above.
Results may differ from the reference program's by a relative error of at most 0.0001.
Values sent between devices are 32-bit elements; how exact they have to be, the bound alone decides.
No kernel may reach another device: no remote copies, remote signals or barrier semaphores. Data moves between devices by JAX's collectives and lax.ppermute only.
A program may use at most 192 MiB of HBM per device.

```python
import math
import jax
import jax.numpy as jnp
from jax import lax

LAT = 128
LON = 256
HB = 128
NBLK = 16
HOURS = 2048


def symmetric_factor(key, order):
    noise_part = jax.random.normal(key, (order, order), jnp.float32) / jnp.sqrt(order * 1.0)
    result = jnp.eye(order, dtype=jnp.float32) + 0.3 * (noise_part + noise_part.T)
    return jnp.clip(result, -1.0, 2.5)


def draw_lat_factor(key, part):
    return symmetric_factor(jax.random.fold_in(key, 11), LAT)


def draw_lon_factor(key, part):
    return symmetric_factor(jax.random.fold_in(key, 13), LON)


def draw_time_tiles(key, part):
    diagonal_tile = symmetric_factor(jax.random.fold_in(key, 21), HB)
    others = 0.5 * jax.random.normal(jax.random.fold_in(key, 22), (4, HB, HB), jnp.float32) / jnp.sqrt(HB * 1.0)
    others = jnp.clip(others, -1.0, 2.5)
    return jnp.concatenate([diagonal_tile[None], others], axis=0)


def with_ends(entries, key, least, top_value):
    longest = entries.shape.index(max(entries.shape))
    spots = []
    for shift in (0, 1):
        where = [jax.random.randint(jax.random.fold_in(key, axis), (), 0, length) for axis, length in enumerate(entries.shape)]
        where[longest] = (where[longest] + shift) % entries.shape[longest]
        spots.append(tuple(where))
    return entries.at[spots[0]].set(least).at[spots[1]].set(top_value)


def shard_levels(own_key, dims, shards, least, top_value):
    factor_of, own = 1.0, jax.random.fold_in(own_key, 6)
    for position, blocks in shards:
        steps = jnp.exp(jax.random.uniform(jax.random.fold_in(own, position), (blocks,), jnp.float32, least / len(shards), top_value / len(shards)))
        factor_of = factor_of * jnp.repeat(steps, dims[position] // blocks).reshape([-1 if axis == position else 1 for axis in range(len(dims))])
    return factor_of


def gaussian(stream_key, shape, deviation, bound, pieces=(), kind=jnp.bfloat16):
    drawn = jax.random.normal(stream_key, shape, jnp.float32) * deviation
    if len(pieces) > 0:
        drawn = shard_levels(stream_key, shape, pieces, -0.22, 0.18) * drawn
    return jnp.clip(drawn, min=-bound, max=bound).astype(kind)


def setup_inputs(seed: int = 0) -> dict:
    arg_keys = jax.random.split(jax.random.key(seed), 9)
    field = gaussian(arg_keys[0], (HOURS, LAT, LON), 1.0, 6.0, ((0, 4), (1, 8)), jnp.float32)
    mask = with_ends((jax.random.randint(arg_keys[1], (HOURS, LAT, LON), 0, 4) < 3).astype(jnp.int32), jax.random.fold_in(arg_keys[1], 1), 0, 1)
    noise = jnp.clip(jnp.exp(math.log(1.0) - 2.3025851 * jax.random.uniform(arg_keys[2], (LAT, LON), jnp.float32) ** shard_levels(arg_keys[2], (LAT, LON), ((0, 8),), -0.2, 0.2)), 0.1, 1.0)
    lat_factor = draw_lat_factor(jax.random.fold_in(arg_keys[8], 71), 0)
    lon_factor = draw_lon_factor(jax.random.fold_in(arg_keys[8], 71), 0)
    time_tiles = draw_time_tiles(jax.random.fold_in(arg_keys[8], 71), 0)
    amplitude = jnp.clip(jnp.exp(jax.random.uniform(arg_keys[6], (NBLK,), jnp.float32, math.log(0.5), math.log(2.0))), 0.5, 2.0)
    depth = with_ends(jax.random.randint(arg_keys[7], (NBLK,), 0, 5), jax.random.fold_in(arg_keys[7], 1), 0, 4).astype(jnp.int32)
    return {"field": field, "mask": mask, "noise": noise, "lat_factor": lat_factor, "lon_factor": lon_factor, "time_tiles": time_tiles, "amplitude": amplitude, "depth": depth}


def band(padded, depth_pad, first_block, block_count, time_tiles):
    highest = lax.Precision.HIGHEST
    result = jnp.einsum("ij,bjs->bis", time_tiles[0], padded[4:4 + block_count], precision=highest)
    for offset in range(1, 5):
        depth_here = lax.dynamic_slice_in_dim(depth_pad, first_block + 4, block_count)
        depth_before = lax.dynamic_slice_in_dim(depth_pad, first_block + 4 - offset, block_count)
        weight_above = (depth_here >= offset).astype(jnp.float32)
        weight_below = (depth_before >= offset).astype(jnp.float32)
        above_term = jnp.einsum("ij,bjs->bis", time_tiles[offset], padded[4 + offset:4 + offset + block_count], precision=highest)
        below_term = jnp.einsum("ji,bjs->bis", time_tiles[offset], padded[4 - offset:4 - offset + block_count], precision=highest)
        result = result + weight_above[:, None, None] * above_term + weight_below[:, None, None] * below_term
    return result


def reference(field, mask, noise, lat_factor, lon_factor, time_tiles, amplitude, depth):
    highest = lax.Precision.HIGHEST
    masked = mask.astype(jnp.float32) * field
    rows_done = jnp.einsum("him,lm->hil", masked, lon_factor, precision=highest)
    columns = jnp.einsum("ij,hjl->hil", lat_factor, rows_done, precision=highest)
    blocks = HOURS // HB
    scaled = columns.reshape(blocks, HB, LAT * LON) * amplitude[:, None, None]
    padded = jnp.pad(scaled, ((4, 4), (0, 0), (0, 0)))
    depth_pad = jnp.pad(depth, 4)
    banded = band(padded, depth_pad, 0, blocks, time_tiles) * amplitude[:, None, None]
    banded = banded.reshape(HOURS, LAT, LON)
    return mask.astype(jnp.float32) * banded + noise[None] * field
```

```python
import functools

import jax
import jax.numpy as jnp
from jax import lax
from jax.experimental import pallas as pl
from jax.experimental.pallas import tpu as pltpu
from jax.sharding import PartitionSpec as P

F32, BF16 = jnp.float32, jnp.bfloat16
MIB = 1 << 20
CHUNKS = 2
LANES = 128


def split(x):
    high = x.astype(BF16)
    return high, (x - high.astype(F32)).astype(BF16)


def halves(x):
    high = lax.reduce_precision(x, 8, 7)
    return high.astype(BF16), lax.reduce_precision(x - high, 8, 7).astype(BF16)


def params(mib):
    return pltpu.CompilerParams(vmem_limit_bytes=mib * MIB)


def cost(flops, nbytes):
    return pl.CostEstimate(flops=int(flops), bytes_accessed=int(nbytes), transcendentals=0)


def head_kernel(lats, field_ref, mask_ref, lon_ref, out_ref, masked):
    hours = field_ref.shape[0] // lats
    cols = out_ref.shape[0] // lats
    for tile in range(masked.shape[0]):
        lanes = slice(tile * LANES, (tile + 1) * LANES)
        masked[tile] = mask_ref[:, lanes].astype(F32) * field_ref[:, lanes]
    weights = lon_ref[...]
    for i in range(lats):
        strided = pl.ds(i, hours, stride=lats)
        tiles = [masked[tile, strided, :] for tile in range(masked.shape[0])]
        high, low = split(jnp.concatenate(tiles, axis=1))
        rows = jnp.concatenate([high, low, high], axis=1)
        out_ref[pl.ds(i, cols, stride=lats), :] = lax.dot_general(
            weights, rows, (((1,), (1,)), ((), ())), preferred_element_type=F32
        )


def head(field, mask, lon3, lats, hour_block):
    rows, lon = field.shape
    hours = rows // lats
    cols = lon3.shape[0]
    return pl.pallas_call(
        functools.partial(head_kernel, lats),
        grid=(hours // hour_block,),
        in_specs=[
            pl.BlockSpec((hour_block * lats, lon), lambda t: (t, 0)),
            pl.BlockSpec((hour_block * lats, lon), lambda t: (t, 0)),
            pl.BlockSpec(lon3.shape, lambda t: (0, 0)),
        ],
        out_specs=pl.BlockSpec((cols * lats, hour_block), lambda t: (0, t)),
        out_shape=jax.ShapeDtypeStruct((cols * lats, hours), F32),
        scratch_shapes=[pltpu.VMEM((lon // LANES, hour_block * lats, LANES), F32)],
        compiler_params=params(40),
        cost_estimate=cost(6 * rows * lon * cols, 4 * rows * (2 * lon + cols)),
        name="head",
    )(field, mask, lon3)


def lat_kernel(x_ref, lat_ref, out_ref):
    parts, count, lats, hours = x_ref.shape
    weights = lat_ref[...]
    for j in range(count):
        high, low = split(x_ref[:, j].reshape(parts * lats, hours))
        rows = jnp.concatenate([high, low, high], axis=0)
        product = jnp.dot(weights, rows, preferred_element_type=F32)
        out_ref[:, j] = product.reshape(parts, lats, hours)


def lat_products(x, lat3):
    parts, count, lats, hours = x.shape
    block = min(count, 4)
    spec = pl.BlockSpec((parts, block, lats, hours), lambda j: (0, j, 0, 0))
    return pl.pallas_call(
        lat_kernel,
        grid=(count // block,),
        in_specs=[spec, pl.BlockSpec(lat3.shape, lambda j: (0, 0))],
        out_specs=spec,
        out_shape=jax.ShapeDtypeStruct(x.shape, F32),
        compiler_params=params(40),
        cost_estimate=cost(6 * x.size * parts * lats, 8 * x.size),
        name="lat",
    )(x, lat3)


def time_kernel(wide, below_ref, own_ref, above_ref, high_ref, low_ref, out_ref):
    reach = below_ref.shape[1]
    hours = own_ref.shape[1]
    padded = jnp.concatenate([below_ref[...], own_ref[...], above_ref[...]], axis=1)
    high, low = split(padded)
    for start in range(0, hours, wide):
        near = slice(start, start + wide + 2 * reach)
        columns = slice(start, start + wide)
        out_ref[:, columns] = (
            jnp.dot(high[:, near], high_ref[near, columns], preferred_element_type=F32)
            + jnp.dot(low[:, near], high_ref[near, columns], preferred_element_type=F32)
            + jnp.dot(high[:, near], low_ref[near, columns], preferred_element_type=F32)
        )


def time_products(below, own, above, high, low):
    rows, hours = own.shape
    reach = below.shape[1]
    block = min(rows, 256)
    wide = min(hours, 256)
    side = pl.BlockSpec((block, reach), lambda r: (r, 0))
    spec = pl.BlockSpec((block, hours), lambda r: (r, 0))
    whole = pl.BlockSpec(high.shape, lambda r: (0, 0))
    return pl.pallas_call(
        functools.partial(time_kernel, wide),
        grid=(rows // block,),
        in_specs=[side, spec, side, whole, whole],
        out_specs=spec,
        out_shape=jax.ShapeDtypeStruct((rows, hours), F32),
        compiler_params=params(40),
        cost_estimate=cost(6 * rows * hours * (wide + 2 * reach), 4 * rows * (2 * hours + 2 * reach)),
        name="time",
    )(below, own, above, high, low)


def band_matrix(time_tiles, amplitude, depth, first, blocks):
    offsets, hb, _ = time_tiles.shape
    reach = offsets - 1
    amp = lax.dynamic_slice_in_dim(jnp.pad(amplitude, reach), first, blocks + 2 * reach)
    dep = lax.dynamic_slice_in_dim(jnp.pad(depth, reach), first, blocks + 2 * reach)
    flipped = jnp.swapaxes(time_tiles, 1, 2)
    columns = []
    for b in range(blocks):
        own = b + reach
        tiles = []
        for r in range(blocks + 2 * reach):
            k = r - own
            if abs(k) > reach:
                tiles.append(jnp.zeros((hb, hb), F32))
                continue
            kept = (abs(k) <= dep[min(r, own)]).astype(F32)
            tile = flipped[k] if k >= 0 else time_tiles[-k]
            tiles.append((kept * amp[own] * amp[r]) * tile)
        columns.append(jnp.concatenate(tiles, axis=0))
    return halves(jnp.concatenate(columns, axis=1))


def tail_kernel(lats, z_ref, field_ref, mask_ref, noise_ref, *rest):
    out_ref, turned = rest[-2], rest[-1]
    cols = z_ref.shape[0] // lats
    hours = z_ref.shape[1]
    for i in range(lats):
        turned[pl.ds(i, hours, stride=lats), :] = z_ref[pl.ds(i, cols, stride=lats), :].T
    shape = (hours, lats, cols)
    out_ref[...] = (
        mask_ref[...].astype(F32).reshape(shape) * turned[...].reshape(shape)
        + noise_ref[...][None] * field_ref[...].reshape(shape)
    ).reshape(hours * lats, cols)


def tail(z, field, mask, noise, before, chunk, lats, hour_block):
    rows, lon = field.shape
    cols = z.shape[0] // lats
    hours = z.shape[1]
    spec = pl.BlockSpec((hour_block * lats, cols), lambda t: (t, chunk))
    operands = [z, field, mask, noise]
    in_specs = [
        pl.BlockSpec((cols * lats, hour_block), lambda t: (0, t)),
        spec,
        spec,
        pl.BlockSpec((lats, cols), lambda t: (0, chunk)),
    ]
    aliases = {}
    if before is not None:
        operands.append(before)
        in_specs.append(pl.BlockSpec(memory_space=pl.ANY))
        aliases = {4: 0}
    return pl.pallas_call(
        functools.partial(tail_kernel, lats),
        grid=(hours // hour_block,),
        in_specs=in_specs,
        out_specs=spec,
        out_shape=jax.ShapeDtypeStruct((rows, lon), F32),
        scratch_shapes=[pltpu.VMEM((hour_block * lats, cols), F32)],
        input_output_aliases=aliases,
        compiler_params=params(40),
        cost_estimate=cost(4 * rows * cols, 16 * rows * cols),
        name="tail",
    )(*operands)


def neighbour(value, steps):
    count = lax.axis_size("tm")
    pairs = [(i, i + steps) for i in range(count) if 0 <= i + steps < count]
    return lax.ppermute(value, "tm", pairs)


def per_device(field, mask, noise, lat_factor, lon_factor, time_tiles, amplitude, depth):
    hours, lats, lon = field.shape
    hb = time_tiles.shape[1]
    reach = (time_tiles.shape[0] - 1) * hb
    parts = lax.axis_size("space")
    width = lon // CHUNKS
    count = width // parts
    field = field.reshape(hours * lats, lon)
    mask = mask.reshape(hours * lats, lon)
    first = lax.axis_index("tm") * (hours // hb)
    lon_high, lon_low = halves(lon_factor)
    lat_high, lat_low = halves(lat_factor)
    lon3 = jnp.concatenate([lon_high, lon_high, lon_low], axis=1)
    lat3 = jnp.concatenate([lat_high, lat_high, lat_low], axis=1)
    band_high, band_low = band_matrix(time_tiles, amplitude, depth, first, hours // hb)
    out = None
    for chunk in range(CHUNKS):
        rows_done = head(field, mask, lon3[chunk * width : (chunk + 1) * width], lats, hb)
        rows_done = rows_done.reshape(parts, count, lats, hours)
        columns = lat_products(
            lax.all_to_all(rows_done, "space", split_axis=0, concat_axis=0, tiled=True), lat3
        ).reshape(width * lats, hours)
        below = neighbour(columns[:, hours - reach :], 1)
        above = neighbour(columns[:, :reach], -1)
        banded = time_products(below, columns, above, band_high, band_low)
        banded = lax.all_to_all(
            banded.reshape(parts, count, lats, hours), "space", split_axis=0, concat_axis=0, tiled=True
        )
        out = tail(banded.reshape(width * lats, hours), field, mask, noise, out, chunk, lats, hb)
    return out.reshape(hours, lats, lon)


def solution(mesh):
    in_specs = (
        P("tm", "space", None),
        P("tm", "space", None),
        P("space", None),
        P(),
        P(),
        P(),
        P(),
        P(),
    )
    out_specs = P("tm", "space", None)
    return jax.shard_map(
        per_device, mesh=mesh, in_specs=in_specs, out_specs=out_specs, check_vma=False
    )
```

```python
import functools

import jax
import jax.numpy as jnp
from jax import lax
from jax.experimental import pallas as pl
from jax.experimental.pallas import tpu as pltpu
from jax.sharding import PartitionSpec as P

F32, BF16 = jnp.float32, jnp.bfloat16
MIB = 1 << 20
CHUNKS = 2
LANES = 128
VMEM = 60
THERE, BACK = ("one", "all"), ("all", "one")


def split(x):
    high = x.astype(BF16)
    return high, (x - high.astype(F32)).astype(BF16)


def params(mib):
    return pltpu.CompilerParams(vmem_limit_bytes=mib * MIB)


def cost(flops, nbytes):
    return pl.CostEstimate(flops=int(flops), bytes_accessed=int(nbytes), transcendentals=0)


def pieces_of(refs):
    near, *far = refs
    return [near.at[d] for d in range(near.shape[0])] + far


def piece_specs(parts, stack, block, index):
    near = pl.BlockSpec((stack, *block), lambda *args: (0, *index(*args)))
    return [near] + [pl.BlockSpec(block, index)] * (parts - stack)


def piece_shapes(parts, stack, shape):
    near = jax.ShapeDtypeStruct((stack, *shape), F32)
    return [near] + [jax.ShapeDtypeStruct(shape, F32)] * (parts - stack)


def sizes_of(pieces):
    stack, rows, hours = pieces[0].shape
    return stack + len(pieces) - 1, stack, rows, hours


def head_kernel(lats, parts, stacks, order_ref, field_ref, mask_ref, lon_ref, *rest):
    masked, weights = rest[-2:]
    outs, used = [], 0
    for stack in stacks:
        arrays = 1 + parts - stack
        outs += pieces_of(rest[used : used + arrays])
        used += arrays
    hours = field_ref.shape[0] // lats
    count = outs[0].shape[0] // lats

    @pl.when(pl.program_id(0) == 0)
    def _():
        for k in range(len(outs)):
            start = pl.multiple_of((k // parts * parts + order_ref[k]) * count, 8)
            high, low = split(lon_ref[pl.ds(start, count), :])
            weights[k] = jnp.concatenate([high, high, low], axis=1)

    for tile in range(masked.shape[0]):
        lanes = slice(tile * LANES, (tile + 1) * LANES)
        masked[tile] = mask_ref[:, lanes].astype(F32) * field_ref[:, lanes]
    lon3 = weights[...].reshape(len(outs) * count, weights.shape[2])

    @pl.loop(0, lats, step=2, unroll=2)
    def _(i):
        lat_rows = []
        for own in (i, i + 1):
            strided = pl.ds(own, hours, stride=lats)
            tiles = [masked[tile, strided, :] for tile in range(masked.shape[0])]
            lat_rows.append(jnp.concatenate(tiles, axis=1))
        high, low = split(jnp.concatenate(lat_rows, axis=0))
        rows = jnp.concatenate([high, low, high], axis=1)
        product = lax.dot_general(lon3, rows, (((1,), (1,)), ((), ())), preferred_element_type=F32)
        for k, out_ref in enumerate(outs):
            part = product[k * count : (k + 1) * count]
            out_ref[pl.ds(i, count, stride=lats), :] = part[:, :hours]
            out_ref[pl.ds(i + 1, count, stride=lats), :] = part[:, hours:]


def head(order, stacks, field, mask, lon_factor, parts, lats, hour_block):
    rows, lon = field.shape
    hours = rows // lats
    count = lon // len(stacks) // parts
    pieces = pl.pallas_call(
        functools.partial(head_kernel, lats, parts, stacks),
        grid_spec=pltpu.PrefetchScalarGridSpec(
            num_scalar_prefetch=1,
            grid=(hours // hour_block,),
            in_specs=[
                pl.BlockSpec((hour_block * lats, lon), lambda t, order: (t, 0)),
                pl.BlockSpec((hour_block * lats, lon), lambda t, order: (t, 0)),
                pl.BlockSpec((lon, lon), lambda t, order: (0, 0)),
            ],
            out_specs=[
                spec
                for stack in stacks
                for spec in piece_specs(parts, stack, (count * lats, hour_block), lambda t, order: (0, t))
            ],
            scratch_shapes=[
                pltpu.VMEM((lon // LANES, hour_block * lats, LANES), F32),
                pltpu.VMEM((len(stacks) * parts, count, 3 * lon), BF16),
            ],
        ),
        out_shape=[
            shape for stack in stacks for shape in piece_shapes(parts, stack, (count * lats, hours))
        ],
        compiler_params=params(VMEM),
        cost_estimate=cost(6 * rows * lon * lon, 12 * rows * lon),
        name="head",
    )(order, field, mask, lon_factor)
    result = []
    for stack in stacks:
        result.append(list(pieces[: 1 + parts - stack]))
        pieces = pieces[1 + parts - stack :]
    return result


def lat_kernel(lats, came_ref, goes_ref, *refs):
    *arrays, lat_ref, out_ref, turned, weights = refs
    parts = pieces_of(arrays)
    block = out_ref.shape[1]

    @pl.when(pl.program_id(0) == 0)
    def _():
        def ordered(ref, order_ref):
            starts = [pl.multiple_of(order_ref[d] * lats, 8) for d in range(len(parts))]
            return jnp.concatenate([ref[pl.ds(start, lats), :] for start in starts], axis=0)

        turned[...] = ordered(lat_ref, came_ref).T
        high, low = split(ordered(turned, goes_ref))
        weights[...] = jnp.concatenate([high, high, low], axis=1)

    @pl.loop(0, block, unroll=2)
    def _(j):
        rows = pl.ds(pl.multiple_of(j * lats, 8), lats)
        high, low = split(jnp.concatenate([part[rows, :] for part in parts], axis=0))
        product = jnp.dot(
            weights[...], jnp.concatenate([high, low, high], axis=0), preferred_element_type=F32
        )
        out_ref[:, j] = product.reshape(len(parts), lats, product.shape[1])


def lat_products(came, goes, pieces, lat_factor, lats):
    parts, stack, rows, hours = sizes_of(pieces)
    count = rows // lats
    block = min(count, 4)
    size = parts * rows * hours
    return pl.pallas_call(
        functools.partial(lat_kernel, lats),
        grid_spec=pltpu.PrefetchScalarGridSpec(
            num_scalar_prefetch=2,
            grid=(count // block,),
            in_specs=[
                *piece_specs(parts, stack, (block * lats, hours), lambda j, *_: (j, 0)),
                pl.BlockSpec(lat_factor.shape, lambda j, *_: (0, 0)),
            ],
            out_specs=pl.BlockSpec((parts, block, lats, hours), lambda j, *_: (0, j, 0, 0)),
            scratch_shapes=[
                pltpu.VMEM(lat_factor.shape, F32),
                pltpu.VMEM((parts * lats, 3 * parts * lats), BF16),
            ],
        ),
        out_shape=jax.ShapeDtypeStruct((parts, count, lats, hours), F32),
        compiler_params=params(VMEM),
        cost_estimate=cost(6 * size * parts * lats, 8 * size),
        name="lat",
    )(came, goes, *pieces, lat_factor)


def time_kernel(
    first_ref, amplitude_ref, depth_ref, below_ref, own_ref, above_ref, tiles_ref, *rest
):
    *arrays, padded_high, padded_low, band_high, band_low = rest
    outs = pieces_of(arrays)
    rows, wide = outs[0].shape
    hb = tiles_ref.shape[1]
    reach = tiles_ref.shape[0] - 1
    steps, near, _ = band_high.shape
    pair = wide // hb
    step = pl.program_id(1)

    @pl.when((pl.program_id(0) == 0) & (step == 0))
    def _():
        band_high[...] = jnp.zeros_like(band_high)
        band_low[...] = jnp.zeros_like(band_low)

        @pl.loop(0, steps * pair)
        def _(b):
            here = first_ref[0] + b
            lane = pl.ds(pl.multiple_of(b % pair * hb, hb), hb)

            def put(k, tile):
                there = jnp.clip(here + k, 0, depth_ref.shape[0] - 1)
                kept = (there == here + k) & (abs(k) <= depth_ref[jnp.minimum(here, there)])
                weight = jnp.where(kept, amplitude_ref[here] * amplitude_ref[there], 0.0)
                high, low = split(weight * tile)
                row = pl.ds(pl.multiple_of((b % pair + reach + k) * hb, hb), hb)
                band_high[b // pair, row, lane] = high
                band_low[b // pair, row, lane] = low

            @pl.loop(0, reach + 1)
            def _(k):
                put(k, tiles_ref[k].T)

            @pl.loop(1, reach + 1)
            def _(k):
                put(-k, tiles_ref[k])

    @pl.when(step == 0)
    def _():
        sides = [ref[...].reshape(len(outs) * rows, ref.shape[3]) for ref in (below_ref, own_ref, above_ref)]
        padded_high[...], padded_low[...] = split(jnp.concatenate(sides, axis=1))

    lanes = pl.ds(pl.multiple_of(step * wide, wide), near)
    high = padded_high[:, lanes]
    product = (
        jnp.dot(high, band_high[step], preferred_element_type=F32)
        + jnp.dot(padded_low[:, lanes], band_high[step], preferred_element_type=F32)
        + jnp.dot(high, band_low[step], preferred_element_type=F32)
    )
    for d, out_ref in enumerate(outs):
        out_ref[...] = product[d * rows : (d + 1) * rows]


def time_products(stack, first, amplitude, depth, below, own, above, time_tiles):
    parts, count, lats, hours = own.shape
    reach = below.shape[3]
    block = min(count, 4)
    wide = min(hours, 2 * time_tiles.shape[1])
    near = wide + 2 * reach
    rows = parts * block * lats
    side = pl.BlockSpec((parts, block, lats, reach), lambda r, s, *_: (0, r, 0, 0))
    spec = pl.BlockSpec((parts, block, lats, hours), lambda r, s, *_: (0, r, 0, 0))
    return pl.pallas_call(
        time_kernel,
        grid_spec=pltpu.PrefetchScalarGridSpec(
            num_scalar_prefetch=3,
            grid=(count // block, hours // wide),
            in_specs=[side, spec, side, pl.BlockSpec(time_tiles.shape, lambda r, s, *_: (0, 0, 0))],
            out_specs=piece_specs(parts, stack, (block * lats, wide), lambda r, s, *_: (r, s)),
            scratch_shapes=[
                pltpu.VMEM((rows, hours + 2 * reach), BF16),
                pltpu.VMEM((rows, hours + 2 * reach), BF16),
                pltpu.VMEM((hours // wide, near, wide), BF16),
                pltpu.VMEM((hours // wide, near, wide), BF16),
            ],
        ),
        out_shape=piece_shapes(parts, stack, (count * lats, hours)),
        compiler_params=params(VMEM),
        cost_estimate=cost(6 * own.size * near, 8 * own.size + 8 * own.size // hours * reach),
        name="time",
    )(first, amplitude, depth, below, own, above, time_tiles)


def tail_kernel(lats, parts, stack, order_ref, *refs):
    arrays = 1 + parts - stack
    pieces = pieces_of(refs[:arrays])
    field_ref, mask_ref, noise_ref = refs[arrays : arrays + 3]
    out_ref, gathered, turned = refs[-3:]
    count = pieces[0].shape[0] // lats
    hours = pieces[0].shape[1]
    for i in range(lats):
        for d, piece in enumerate(pieces):
            start = pl.multiple_of((order_ref[d]) * count, 8)
            gathered[i, pl.ds(start, count), :] = piece[pl.ds(i, count, stride=lats), :]
        turned[pl.ds(i, hours, stride=lats), :] = gathered[i].T
    shape = (hours, lats, parts * count)
    out_ref[...] = (
        mask_ref[...].astype(F32).reshape(shape) * turned[...].reshape(shape)
        + noise_ref[...][None] * field_ref[...].reshape(shape)
    ).reshape(out_ref.shape)


def tail(order, pieces, field, mask, noise, before, chunk, lats, hour_block):
    rows, lon = field.shape
    parts, stack, piece_rows, hours = sizes_of(pieces)
    width = parts * piece_rows // lats
    spec = pl.BlockSpec((hour_block * lats, width), lambda t, order: (t, chunk))
    operands = [order, *pieces, field, mask, noise]
    in_specs = [
        *piece_specs(parts, stack, (piece_rows, hour_block), lambda t, order: (0, t)),
        spec,
        spec,
        pl.BlockSpec((lats, width), lambda t, order: (0, chunk)),
    ]
    aliases = {}
    if before is not None:
        aliases = {len(operands): 0}
        operands.append(before)
        in_specs.append(pl.BlockSpec(memory_space=pl.ANY))
    return pl.pallas_call(
        functools.partial(tail_kernel, lats, parts, stack),
        grid_spec=pltpu.PrefetchScalarGridSpec(
            num_scalar_prefetch=1,
            grid=(hours // hour_block,),
            in_specs=in_specs,
            out_specs=spec,
            scratch_shapes=[
                pltpu.VMEM((lats, width, hour_block), F32),
                pltpu.VMEM((hour_block * lats, width), F32),
            ],
        ),
        out_shape=jax.ShapeDtypeStruct((rows, lon), F32),
        input_output_aliases=aliases,
        compiler_params=params(VMEM),
        cost_estimate=cost(4 * rows * width, 16 * rows * width),
        name="tail",
    )(*operands)


def neighbour(value, steps):
    count = lax.axis_size("tm")
    pairs = [(i, i + steps) for i in range(count) if 0 <= i + steps < count]
    return lax.ppermute(value, "tm", pairs)


def after(value, *earlier):
    return lax.optimization_barrier((value, *earlier))[0]


def exchange(pieces):
    parts, stack, _, _ = sizes_of(pieces)
    if stack == parts:
        return [lax.all_to_all(pieces[0], "space", split_axis=0, concat_axis=0, tiled=True)]
    result = list(pieces)
    for d in reversed(range(1, parts)):
        result[d] = lax.ppermute(pieces[d], "space", [(i, i ^ d) for i in range(parts)])
    return result


def per_device(field, mask, noise, lat_factor, lon_factor, time_tiles, amplitude, depth):
    hours, lats, lon = field.shape
    hb = time_tiles.shape[1]
    reach = (time_tiles.shape[0] - 1) * hb
    parts = lax.axis_size("space")
    field = field.reshape(hours * lats, lon)
    mask = mask.reshape(hours * lats, lon)
    place = lax.axis_index("space")
    first = (lax.axis_index("tm") * (hours // hb)).astype(jnp.int32).reshape(1)
    there = [1 if name == "one" else parts for name in THERE]
    back = [1 if name == "one" else parts for name in BACK]
    order = {1: place ^ jnp.arange(parts), parts: jnp.arange(parts)}
    order = {stack: which.astype(jnp.int32) for stack, which in order.items()}
    heads = jnp.concatenate([order[stack] for stack in there])
    sent = head(heads, there, field, mask, lon_factor, parts, lats, hb)
    arrived = [exchange(sent[0])]
    for pieces in sent[1:]:
        pieces[0] = after(pieces[0], *arrived[-1][1:])
        arrived.append(exchange(pieces))
    returned = []
    for c in range(CHUNKS):
        if c > 0:
            arrived[c][0] = after(arrived[c][0], banded[0])
        columns = lat_products(order[there[c]], order[back[c]], arrived[c], lat_factor, lats)
        below = neighbour(columns[..., hours - reach :], 1)
        above = neighbour(columns[..., :reach], -1)
        banded = time_products(back[c], first, amplitude, depth, below, columns, above, time_tiles)
        returned.append(exchange(banded))
    out = None
    for c in range(CHUNKS):
        if c == 0:
            returned[c][0] = after(returned[c][0], banded[0])
        out = tail(order[back[c]], returned[c], field, mask, noise, out, c, lats, hb)
    return out.reshape(hours, lats, lon)


def solution(mesh):
    in_specs = (
        P("tm", "space", None),
        P("tm", "space", None),
        P("space", None),
        P(),
        P(),
        P(),
        P(),
        P(),
    )
    out_specs = P("tm", "space", None)
    return jax.shard_map(
        per_device, mesh=mesh, in_specs=in_specs, out_specs=out_specs, check_vma=False
    )
```

```python
import functools

import jax
import jax.numpy as jnp
from jax import lax
from jax.experimental import pallas as pl
from jax.experimental.pallas import tpu as pltpu
from jax.sharding import PartitionSpec as P

F32, BF16 = jnp.float32, jnp.bfloat16
MIB = 1 << 20
CHUNKS = 2
LANES = 128
VMEM = 60
def sends(blocks):
    return [(0, 0, EARLY, True), (0, EARLY, blocks, False), (1, 0, blocks, True)]


EARLY = 1
RETURNS = [[True], [False]]


def split(x):
    high = x.astype(BF16)
    return high, (x - high.astype(F32)).astype(BF16)


def params(mib):
    return pltpu.CompilerParams(vmem_limit_bytes=mib * MIB)


def cost(flops, nbytes):
    return pl.CostEstimate(flops=int(flops), bytes_accessed=int(nbytes), transcendentals=0)


def pieces_of(refs, order_ref):
    if len(refs) > 1:
        return list(refs)
    return [refs[0].at[order_ref[d]] for d in range(refs[0].shape[0])]


def piece_specs(parts, stacked, block, index):
    if stacked:
        return [pl.BlockSpec((parts, *block), lambda *args: (0, *index(*args)))]
    return [pl.BlockSpec(block, index)] * parts


def piece_shapes(parts, stacked, shape):
    if stacked:
        return [jax.ShapeDtypeStruct((parts, *shape), F32)]
    return [jax.ShapeDtypeStruct(shape, F32)] * parts


def sizes_of(pieces):
    stacked = len(pieces) == 1
    return pieces[0].shape[0] if stacked else len(pieces), stacked, *pieces[0].shape[-2:]


def head_kernel(lats, order_ref, field_ref, mask_ref, lon_ref, *rest):
    masked, weights = rest[-2:]
    outs = pieces_of(rest[:-2], order_ref)
    hours = field_ref.shape[0] // lats
    count = outs[0].shape[0] // lats

    @pl.when(pl.program_id(0) == 0)
    def _():
        for d in range(len(outs)):
            start = pl.multiple_of(order_ref[d] * count, 8)
            high, low = split(lon_ref[pl.ds(start, count), :])
            weights[d] = jnp.concatenate([high, high, low], axis=1)

    for tile in range(masked.shape[0]):
        lanes = slice(tile * LANES, (tile + 1) * LANES)
        masked[tile] = mask_ref[:, lanes].astype(F32) * field_ref[:, lanes]
    lon3 = weights[...].reshape(len(outs) * count, weights.shape[2])

    @pl.loop(0, lats, step=2, unroll=2)
    def _(i):
        lat_rows = []
        for own in (i, i + 1):
            strided = pl.ds(own, hours, stride=lats)
            tiles = [masked[tile, strided, :] for tile in range(masked.shape[0])]
            lat_rows.append(jnp.concatenate(tiles, axis=1))
        high, low = split(jnp.concatenate(lat_rows, axis=0))
        rows = jnp.concatenate([high, low, high], axis=1)
        product = lax.dot_general(lon3, rows, (((1,), (1,)), ((), ())), preferred_element_type=F32)
        for d, out_ref in enumerate(outs):
            part = product[d * count : (d + 1) * count]
            out_ref[pl.ds(i, count, stride=lats), :] = part[:, :hours]
            out_ref[pl.ds(i + 1, count, stride=lats), :] = part[:, hours:]


def head(order, stacked, field, mask, lon_factor, chunk, blocks, lats, hour_block):
    first, last = blocks
    lon = field.shape[1]
    hours = (last - first) * hour_block
    parts = order.shape[0]
    width = lon // CHUNKS
    count = width // parts
    rows = hours * lats
    spec = pl.BlockSpec((hour_block * lats, lon), lambda t, order: (first + t, 0))
    return pl.pallas_call(
        functools.partial(head_kernel, lats),
        grid_spec=pltpu.PrefetchScalarGridSpec(
            num_scalar_prefetch=1,
            grid=(last - first,),
            in_specs=[spec, spec, pl.BlockSpec((width, lon), lambda t, order: (chunk, 0))],
            out_specs=piece_specs(parts, stacked, (count * lats, hour_block), lambda t, order: (0, t)),
            scratch_shapes=[
                pltpu.VMEM((lon // LANES, hour_block * lats, LANES), F32),
                pltpu.VMEM((parts, count, 3 * lon), BF16),
            ],
        ),
        out_shape=piece_shapes(parts, stacked, (count * lats, hours)),
        compiler_params=params(VMEM),
        cost_estimate=cost(6 * rows * lon * width, 4 * rows * (2 * lon + width)),
        name="head",
    )(order, field, mask, lon_factor)


def lat_kernel(lats, arrays, order_ref, *refs):
    lat_ref, out_ref, turned, weights = refs[-4:]
    sets, used = [], 0
    for some in arrays:
        sets.append(pieces_of(refs[used : used + some], order_ref))
        used += some
    parts, block = out_ref.shape[:2]

    @pl.when(pl.program_id(0) == 0)
    def _():
        def ordered(ref):
            starts = [pl.multiple_of(order_ref[d] * lats, 8) for d in range(parts)]
            return jnp.concatenate([ref[pl.ds(start, lats), :] for start in starts], axis=0)

        turned[...] = ordered(lat_ref).T
        high, low = split(ordered(turned))
        weights[...] = jnp.concatenate([high, high, low], axis=1)

    @pl.loop(0, block, unroll=2)
    def _(j):
        rows = pl.ds(pl.multiple_of(j * lats, 8), lats)
        values = [jnp.concatenate([piece[rows, :] for piece in pieces], axis=0) for pieces in sets]
        high, low = split(jnp.concatenate(values, axis=1))
        product = jnp.dot(
            weights[...], jnp.concatenate([high, low, high], axis=0), preferred_element_type=F32
        )
        out_ref[:, j] = product.reshape(parts, lats, product.shape[1])


def lat_products(order, sets, lat_factor, lats):
    parts = order.shape[0]
    sizes = [sizes_of(pieces) for pieces in sets]
    count = sizes[0][2] // lats
    hours = sum(size[3] for size in sizes)
    block = min(count, 4)
    size = parts * count * lats * hours
    return pl.pallas_call(
        functools.partial(lat_kernel, lats, [len(pieces) for pieces in sets]),
        grid_spec=pltpu.PrefetchScalarGridSpec(
            num_scalar_prefetch=1,
            grid=(count // block,),
            in_specs=[
                spec
                for _, stacked, _, some in sizes
                for spec in piece_specs(parts, stacked, (block * lats, some), lambda j, order: (j, 0))
            ]
            + [pl.BlockSpec(lat_factor.shape, lambda j, order: (0, 0))],
            out_specs=pl.BlockSpec((parts, block, lats, hours), lambda j, order: (0, j, 0, 0)),
            scratch_shapes=[
                pltpu.VMEM(lat_factor.shape, F32),
                pltpu.VMEM((parts * lats, 3 * parts * lats), BF16),
            ],
        ),
        out_shape=jax.ShapeDtypeStruct((parts, count, lats, hours), F32),
        compiler_params=params(VMEM),
        cost_estimate=cost(6 * size * parts * lats, 8 * size),
        name="lat",
    )(order, *[piece for pieces in sets for piece in pieces], lat_factor)


def time_kernel(
    arrays, order_ref, first_ref, amplitude_ref, depth_ref, below_ref, own_ref, above_ref, tiles_ref, *rest
):
    padded_high, padded_low, band_high, band_low = rest[-4:]
    sets, used = [], 0
    for some in arrays:
        sets.append(pieces_of(rest[used : used + some], order_ref))
        used += some
    parts = own_ref.shape[0]
    rows, wide = sets[0][0].shape
    hb = tiles_ref.shape[1]
    reach = tiles_ref.shape[0] - 1
    steps, near, _ = band_high.shape
    pair = wide // hb
    step = pl.program_id(1)

    @pl.when((pl.program_id(0) == 0) & (step == 0))
    def _():
        band_high[...] = jnp.zeros_like(band_high)
        band_low[...] = jnp.zeros_like(band_low)

        @pl.loop(0, steps * pair)
        def _(b):
            here = first_ref[0] + b
            lane = pl.ds(pl.multiple_of(b % pair * hb, hb), hb)

            def put(k, tile):
                there = jnp.clip(here + k, 0, depth_ref.shape[0] - 1)
                kept = (there == here + k) & (abs(k) <= depth_ref[jnp.minimum(here, there)])
                weight = jnp.where(kept, amplitude_ref[here] * amplitude_ref[there], 0.0)
                high, low = split(weight * tile)
                row = pl.ds(pl.multiple_of((b % pair + reach + k) * hb, hb), hb)
                band_high[b // pair, row, lane] = high
                band_low[b // pair, row, lane] = low

            @pl.loop(0, reach + 1)
            def _(k):
                put(k, tiles_ref[k].T)

            @pl.loop(1, reach + 1)
            def _(k):
                put(-k, tiles_ref[k])

    @pl.when(step == 0)
    def _():
        sides = [ref[...].reshape(parts * rows, ref.shape[3]) for ref in (below_ref, own_ref, above_ref)]
        padded_high[...], padded_low[...] = split(jnp.concatenate(sides, axis=1))

    lanes = pl.ds(pl.multiple_of(step * wide, wide), near)
    high = padded_high[:, lanes]
    product = (
        jnp.dot(high, band_high[step], preferred_element_type=F32)
        + jnp.dot(padded_low[:, lanes], band_high[step], preferred_element_type=F32)
        + jnp.dot(high, band_low[step], preferred_element_type=F32)
    )
    for k, outs in enumerate(sets):

        @pl.when((len(sets) == 1) | (step == k))
        def _():
            for d, out_ref in enumerate(outs):
                out_ref[...] = product[d * rows : (d + 1) * rows]


def time_products(order, stacks, first, amplitude, depth, below, own, above, time_tiles):
    parts, count, lats, hours = own.shape
    reach = below.shape[3]
    block = min(count, 4)
    wide = min(hours, 2 * time_tiles.shape[1])
    near = wide + 2 * reach
    rows = parts * block * lats
    whole = len(stacks) == 1
    side = pl.BlockSpec((parts, block, lats, reach), lambda r, s, *_: (0, r, 0, 0))
    spec = pl.BlockSpec((parts, block, lats, hours), lambda r, s, *_: (0, r, 0, 0))
    index = (lambda r, s, *_: (r, s)) if whole else (lambda r, s, *_: (r, 0))
    shape = (count * lats, hours if whole else wide)
    shapes = [piece_shapes(parts, stacked, shape) for stacked in stacks]
    results = pl.pallas_call(
        functools.partial(time_kernel, [len(some) for some in shapes]),
        grid_spec=pltpu.PrefetchScalarGridSpec(
            num_scalar_prefetch=4,
            grid=(count // block, hours // wide),
            in_specs=[side, spec, side, pl.BlockSpec(time_tiles.shape, lambda r, s, *_: (0, 0, 0))],
            out_specs=[
                out for stacked in stacks for out in piece_specs(parts, stacked, (block * lats, wide), index)
            ],
            scratch_shapes=[
                pltpu.VMEM((rows, hours + 2 * reach), BF16),
                pltpu.VMEM((rows, hours + 2 * reach), BF16),
                pltpu.VMEM((hours // wide, near, wide), BF16),
                pltpu.VMEM((hours // wide, near, wide), BF16),
            ],
        ),
        out_shape=[out for some in shapes for out in some],
        compiler_params=params(VMEM),
        cost_estimate=cost(6 * own.size * near, 8 * own.size + 8 * own.size // hours * reach),
        name="time",
    )(order, first, amplitude, depth, below, own, above, time_tiles)
    sets = []
    for some in shapes:
        sets.append(list(results[: len(some)]))
        results = results[len(some) :]
    return sets


def tail_kernel(lats, arrays, order_ref, *refs):
    pieces = pieces_of(refs[:arrays], order_ref)
    field_ref, mask_ref, noise_ref = refs[arrays : arrays + 3]
    out_ref, gathered, turned = refs[-3:]
    count = pieces[0].shape[0] // lats
    hours = pieces[0].shape[1]

    @pl.loop(0, lats, unroll=4)
    def _(i):
        for d, piece in enumerate(pieces):
            start = pl.multiple_of(order_ref[d] * count, 8)
            gathered[i, pl.ds(start, count), :] = piece[pl.ds(i, count, stride=lats), :]
        turned[pl.ds(i, hours, stride=lats), :] = gathered[i].T

    shape = (hours, lats, len(pieces) * count)
    out_ref[...] = (
        mask_ref[...].astype(F32).reshape(shape) * turned[...].reshape(shape)
        + noise_ref[...][None] * field_ref[...].reshape(shape)
    ).reshape(out_ref.shape)


def tail(order, pieces, field, mask, noise, before, chunk, first, lats, hour_block):
    rows, lon = field.shape
    parts, stacked, piece_rows, hours = sizes_of(pieces)
    width = parts * piece_rows // lats
    spec = pl.BlockSpec((hour_block * lats, width), lambda t, order: (first + t, chunk))
    operands = [order, *pieces, field, mask, noise]
    in_specs = [
        *piece_specs(parts, stacked, (piece_rows, hour_block), lambda t, order: (0, t)),
        spec,
        spec,
        pl.BlockSpec((lats, width), lambda t, order: (0, chunk)),
    ]
    aliases = {}
    if before is not None:
        aliases = {len(operands): 0}
        operands.append(before)
        in_specs.append(pl.BlockSpec(memory_space=pl.ANY))
    return pl.pallas_call(
        functools.partial(tail_kernel, lats, len(pieces)),
        grid_spec=pltpu.PrefetchScalarGridSpec(
            num_scalar_prefetch=1,
            grid=(hours // hour_block,),
            in_specs=in_specs,
            out_specs=spec,
            scratch_shapes=[
                pltpu.VMEM((lats, width, hour_block), F32),
                pltpu.VMEM((hour_block * lats, width), F32),
            ],
        ),
        out_shape=jax.ShapeDtypeStruct((rows, lon), F32),
        input_output_aliases=aliases,
        compiler_params=params(VMEM),
        cost_estimate=cost(4 * hours * lats * width, 16 * hours * lats * width),
        name="tail",
    )(*operands)


def neighbour(value, steps):
    count = lax.axis_size("tm")
    pairs = [(i, i + steps) for i in range(count) if 0 <= i + steps < count]
    return lax.ppermute(value, "tm", pairs)


def after(value, *earlier):
    return lax.optimization_barrier((value, *earlier))[0]


def exchange(pieces):
    if len(pieces) == 1:
        return [lax.all_to_all(pieces[0], "space", split_axis=0, concat_axis=0, tiled=True)]
    parts = len(pieces)
    result = list(pieces)
    for d in reversed(range(1, parts)):
        result[d] = lax.ppermute(pieces[d], "space", [(i, i ^ d) for i in range(parts)])
    return result


def per_device(field, mask, noise, lat_factor, lon_factor, time_tiles, amplitude, depth):
    hours, lats, lon = field.shape
    hb = time_tiles.shape[1]
    reach = (time_tiles.shape[0] - 1) * hb
    parts = lax.axis_size("space")
    field = field.reshape(hours * lats, lon)
    mask = mask.reshape(hours * lats, lon)
    place = lax.axis_index("space")
    first = (lax.axis_index("tm") * (hours // hb)).astype(jnp.int32).reshape(1)
    order = (place ^ jnp.arange(parts)).astype(jnp.int32)
    blocks = hours // hb
    arrived = []
    before = None
    for chunk, first_block, last_block, stacked in sends(blocks):
        part = (first_block, last_block)
        pieces = head(order, stacked, field, mask, lon_factor, chunk, part, lats, hb)
        if before is not None and stacked:
            pieces = [after(pieces[0], *before[1:])]
        before = exchange(pieces)
        arrived.append((chunk, before))
    returned = []
    banded = None
    for chunk in range(CHUNKS):
        sets = [pieces for which, pieces in arrived if which == chunk]
        if banded is not None:
            sets[0] = [after(sets[0][0], banded[0][0])] + sets[0][1:]
        columns = lat_products(order, sets, lat_factor, lats)
        below = neighbour(columns[..., hours - reach :], 1)
        above = neighbour(columns[..., :reach], -1)
        banded = time_products(
            order, RETURNS[chunk], first, amplitude, depth, below, columns, above, time_tiles
        )
        returned.append([exchange(pieces) for pieces in banded])
    out = None
    for chunk in range(CHUNKS):
        start = 0
        for pieces in returned[chunk]:
            if out is None:
                pieces = [after(pieces[0], banded[0][0])] + pieces[1:]
            out = tail(order, pieces, field, mask, noise, out, chunk, start, lats, hb)
            start += pieces[0].shape[-1] // hb
    return out.reshape(hours, lats, lon)


def solution(mesh):
    in_specs = (
        P("tm", "space", None),
        P("tm", "space", None),
        P("space", None),
        P(),
        P(),
        P(),
        P(),
        P(),
    )
    out_specs = P("tm", "space", None)
    return jax.shard_map(
        per_device, mesh=mesh, in_specs=in_specs, out_specs=out_specs, check_vma=False
    )
```
